256 devices in a mesh: pop: 16 (over z, y_lo), tp: 16 (over y_hi, x, core).
Axes of the slice: x: 4, y: 4 (y_hi: 2, y_lo: 2; y = y_hi * 2 + y_lo), z: 8, core: 2. Of those that a mesh axis runs over, the one named last changes fastest.
Arguments:
- tokens: bfloat16 [16384, 5120], P('pop', 'tp'), may hold values from -6 to 6
- weight: bfloat16 [5120, 17408], P(None, 'tp'), may hold values from -0.078125 to 0.078125
- factor_a: bfloat16 [128, 4, 5120], P('pop'), may hold values from -6 to 6
- factor_b: bfloat16 [128, 4, 17408], P('pop', None, 'tp'), may hold values from -6 to 6
- member_of_row: int32 [16384], P('pop'), may hold values from 0 to 127, as said below
- fitness_rank: int32 [128], P('pop'), may hold values from 0 to 127, each once
Outputs:
- activations: bfloat16 [16384, 17408], P('pop', 'tp')
- update: bfloat16 [5120, 17408], P('pop', 'tp')
The draws below stay inside these ranges and needn't reach their ends.
Inputs may be any that keep to these rules, and one draw needn't show every extreme that they name: `member_of_row`: the rows held by index p of pop belong to members p * 8 to (p + 1) * 8 - 1, each member owning exactly 128 of them, in a random order. `fitness_rank`: A permutation of the members' ranks.
All inputs are finite; a program needn't handle non-finite values.
Results may differ from the reference program's by a relative error of at most 0.0049.
Values may be sent and summed in bfloat16 or wider, within the bound.
No kernel may reach another device: no remote copies, remote signals or barrier semaphores. Data moves between devices by JAX's collectives and lax.ppermute only.
A program may use at most 128 MiB of HBM per device.

```python
import math
import jax
import jax.numpy as jnp
from jax import lax

D = 5120
FF = 17408
RANK = 4
TOK_DEV = 1024
MEM_DEV = 8
POP = 128
TOKENS = 16384


def draw_member_of_row(key, part):
    key = jax.random.fold_in(key, 7)
    blocks = TOKENS // TOK_DEV
    base = jnp.repeat(jnp.arange(MEM_DEV, dtype=jnp.int32), TOK_DEV // MEM_DEV)
    keys = jax.random.split(key, blocks)
    shuffled = jax.vmap(lambda single: jax.random.permutation(single, base))(keys)
    offsets = (jnp.arange(blocks, dtype=jnp.int32) * MEM_DEV)[:, None]
    return (shuffled + offsets).reshape(TOKENS).astype(jnp.int32)


def block_levels(stream_key, shape, pieces, least, top_value):
    factor_of = 1.0
    for dim, parts in pieces:
        draws = jax.random.uniform(jax.random.fold_in(jax.random.fold_in(stream_key, 6), dim), (parts,), jnp.float32, least / len(pieces), top_value / len(pieces))
        factor_of = factor_of * jnp.repeat(jnp.exp(draws), shape[dim] // parts).reshape((-1,) + (1,) * (len(shape) - 1 - dim))
    return factor_of


def noise(key, dims, spread, reach, shards=(), held_as=jnp.bfloat16):
    entries = jax.random.normal(key, dims, jnp.float32) * spread
    if len(shards) > 0:
        entries = block_levels(key, dims, shards, -0.22, 0.18) * entries
    return jnp.clip(entries, min=-reach, max=reach).astype(held_as)


def setup_inputs(seed: int = 0) -> dict:
    key_list = jax.random.split(jax.random.key(seed), 7)
    tokens = noise(key_list[0], (TOKENS, D), 1.0, 6.0, ((0, 16), (1, 16)))
    weight = noise(key_list[1], (D, FF), D ** -0.5, 0.078125, ((1, 16),))
    factor_a = noise(key_list[2], (POP, RANK, D), 1.0, 6.0, ((0, 16),))
    factor_b = noise(key_list[3], (POP, RANK, FF), 1.0, 6.0, ((0, 16), (2, 16)))
    member_of_row = draw_member_of_row(jax.random.fold_in(key_list[6], 71), 0)
    fitness_rank = jax.random.permutation(key_list[5], POP).astype(jnp.int32)
    return {"tokens": tokens, "weight": weight, "factor_a": factor_a, "factor_b": factor_b, "member_of_row": member_of_row, "fitness_rank": fitness_rank}


perturb_scale = 0.5

def reference(tokens, weight, factor_a, factor_b, member_of_row, fitness_rank):
    preact = jnp.dot(tokens, weight, preferred_element_type=jnp.float32)

    def block_terms(inputs):
        rows_now, owners = inputs
        a_rows = factor_a[owners].astype(jnp.float32)
        lowrank = jnp.einsum('nd,nrd->nr', rows_now.astype(jnp.float32), a_rows)
        coefficient = (lowrank * (perturb_scale / math.sqrt(D))).astype(jnp.bfloat16)
        b_rows = factor_b[owners].astype(jnp.float32)
        return jnp.einsum('nr,nrf->nf', coefficient.astype(jnp.float32), b_rows)
    correction = lax.map(block_terms, (tokens.reshape(TOKENS // TOK_DEV, TOK_DEV, D), member_of_row.reshape(TOKENS // TOK_DEV, TOK_DEV)))
    correction = correction.reshape(TOKENS, FF)
    activations = jax.nn.silu(preact + correction).astype(jnp.bfloat16)
    fitness = 2.0 * fitness_rank.astype(jnp.float32) / (POP - 1) - 1.0
    scaled_b = (factor_b.astype(jnp.float32) * fitness[:, None, None]).astype(jnp.bfloat16)
    summed = jnp.dot(factor_a.reshape(POP * RANK, D).T, scaled_b.reshape(POP * RANK, FF), preferred_element_type=jnp.float32)
    update = (summed * (1.0 / math.sqrt(POP * RANK))).astype(jnp.bfloat16)
    return (activations, update)
```

```python
import functools
import math

import jax
import jax.numpy as jnp
from jax import lax
from jax.experimental import pallas as pl
from jax.experimental.pallas import tpu as pltpu
from jax.sharding import PartitionSpec as P

perturb_scale = 0.5
f32, bf16 = jnp.float32, jnp.bfloat16

D, COLS, ROWS, SHARD = 5120, 1088, 1024, 320
CHIP = 2 * SHARD
LOW = 32
TALL = COLS + LOW
NB = 256
WIDE = 384
PAY = WIDE + COLS
POPS, XS = 16, 4
VMEM = 56 * 2**20

TP = [(y, x, c) for y in range(2) for x in range(XS) for c in range(2)]


def tp_at(y, x, c):
    return ((y % 2) * XS + x % XS) * 2 + c % 2


X_UP = [(tp_at(y, x, c), tp_at(y, x + 1, c)) for y, x, c in TP]
X_DOWN = [(tp_at(y, x, c), tp_at(y, x - 1, c)) for y, x, c in TP]
Y_SWAP = [(tp_at(y, x, c), tp_at(y + 1, x, c)) for y, x, c in TP]
CORE_SWAP = [(tp_at(y, x, c), tp_at(y, x, c + 1)) for y, x, c in TP]


def cost(flops, nbytes):
    return pl.CostEstimate(flops=int(flops), bytes_accessed=int(nbytes), transcendentals=0)


def load_group(chips, pieces, s, w, a, mine, other, wx, xs, sem):
    copies = []
    for k in range(chips):
        col = pl.multiple_of(s[k] * CHIP, 128)
        copies.append((w.at[:, pl.ds(col, CHIP)], wx.at[pl.ds(0, COLS), pl.ds(k * CHIP, CHIP)]))
        copies.append((a.at[:, pl.ds(col, CHIP)], wx.at[pl.ds(COLS, LOW), pl.ds(k * CHIP, CHIP)]))
    core = s[chips]
    start = 0
    for piece, (m, o) in enumerate(zip(mine, other)):
        chip, within = pieces[piece]
        size = m.shape[0]
        base = chip * CHIP + within
        m_row = pl.multiple_of(base + core * SHARD, 16)
        o_row = pl.multiple_of(base + (1 - core) * SHARD, 16)
        copies.append((m, xs.at[pl.ds(m_row, size), :]))
        copies.append((o, xs.at[pl.ds(o_row, size), :]))
    handles = [pltpu.make_async_copy(src, dst, sem.at[i]) for i, (src, dst) in enumerate(copies)]
    for h in handles:
        h.start()
    for h in handles:
        h.wait()


def group_kernel(chips, pieces, first, last, s, *refs):
    n = len(pieces)
    w, a = refs[0], refs[1]
    mine, other = refs[2 : 2 + n], refs[2 + n : 2 + 2 * n]
    rest = list(refs[2 + 2 * n :])
    acc = None if first else rest.pop(0)
    if last:
        b, member = rest.pop(0), rest.pop(0)
    out, wx, xs, sem = rest
    j = pl.program_id(0)

    @pl.when(j == 0)
    def _():
        load_group(chips, pieces, s, w, a, mine, other, wx, xs, sem)

    cols = pl.ds(pl.multiple_of(j * NB, NB), NB)
    part = jnp.dot(wx[...], xs[:, cols], preferred_element_type=f32)
    if not first:
        part = part + acc[...]
    if not last:
        out[...] = part
        return
    low = part[COLS:, :] * (perturb_scale / math.sqrt(D))
    rank_row = lax.broadcasted_iota(jnp.int32, (LOW, NB), 0) >> 2
    local = member[...] - s[chips + 1] * 8
    coef = jnp.where(rank_row == local, low, 0.0).astype(bf16)
    corr = lax.dot_general(b[...], coef, (((0,), (0,)), ((), ())), preferred_element_type=f32)
    v = part[:COLS, :] + corr
    out[...] = (v * (1.0 / (1.0 + jnp.exp(-v)))).astype(bf16)


def group(chips, pieces, scalars, w, a, mine, other, acc=None, last=None):
    n = len(pieces)
    any_spec = pl.BlockSpec(memory_space=pl.ANY)
    column = pl.BlockSpec((TALL, NB), lambda j, s: (0, j))
    in_specs = [any_spec] * (2 + 2 * n)
    args = [w, a, *mine, *other]
    if acc is not None:
        in_specs.append(column)
        args.append(acc)
    if last is not None:
        in_specs += [
            pl.BlockSpec((LOW, COLS), lambda j, s: (0, 0)),
            pl.BlockSpec((1, NB), lambda j, s: (0, j)),
        ]
        args += list(last)
        out_shape = jax.ShapeDtypeStruct((COLS, ROWS), bf16)
        out_spec = pl.BlockSpec((COLS, NB), lambda j, s: (0, j))
    else:
        out_shape = jax.ShapeDtypeStruct((TALL, ROWS), f32)
        out_spec = column
    depth = chips * CHIP
    return pl.pallas_call(
        functools.partial(group_kernel, chips, pieces, acc is None, last is not None),
        out_shape=out_shape,
        grid_spec=pltpu.PrefetchScalarGridSpec(
            num_scalar_prefetch=1,
            grid=(ROWS // NB,),
            in_specs=in_specs,
            out_specs=out_spec,
            scratch_shapes=[
                pltpu.VMEM((TALL, depth), bf16),
                pltpu.VMEM((depth, ROWS), bf16),
                pltpu.SemaphoreType.DMA((2 * chips + 2 * n,)),
            ],
        ),
        compiler_params=pltpu.CompilerParams(vmem_limit_bytes=VMEM),
        cost_estimate=cost(2 * TALL * depth * ROWS, 2 * depth * (TALL + ROWS) + 8 * TALL * ROWS),
    )(scalars, *args)


def payload_kernel(a, b, fit, out):
    scaled = (b[...].astype(f32) * fit[...]).astype(bf16)
    for p in range(POPS):
        start = (p * SHARD) // 128 * 128
        out[p, :, :WIDE] = a[:, start : start + WIDE]
        out[p, :, WIDE:] = scaled


def update_kernel(s, got, out, wide):
    wide[...] = lax.dot_general(
        got[:, :WIDE], got[:, WIDE:], (((0,), (0,)), ((), ())), preferred_element_type=f32
    )
    first = pl.multiple_of(s[0] * 64, 64)
    out[...] = (wide[pl.ds(first, SHARD), :] * (1.0 / math.sqrt(512))).astype(bf16)


def body(tokens, weight, factor_a, factor_b, member_of_row, fitness_rank):
    pop = lax.axis_index("pop")
    tp = lax.axis_index("tp")
    core, x, y = tp % 2, (tp // 2) % XS, tp // (2 * XS)
    shard = tokens.T
    w = weight.T
    a = factor_a.reshape(LOW, D)
    b = factor_b.reshape(LOW, COLS)

    send = lambda v, perm: lax.ppermute(v, "tp", perm)
    swap = lambda v: send(v, CORE_SWAP)

    low_x = send(shard, X_UP)
    high_x = send(shard, X_DOWN)
    far_y = send(shard, Y_SWAP)
    own_o = swap(shard)

    fitness = 2.0 * fitness_rank.astype(f32) / 127.0 - 1.0
    payload = pl.pallas_call(
        payload_kernel,
        out_shape=jax.ShapeDtypeStruct((POPS, LOW, PAY), bf16),
        compiler_params=pltpu.CompilerParams(vmem_limit_bytes=VMEM),
        cost_estimate=cost(LOW * COLS, POPS * LOW * PAY * 2),
    )(a, b, jnp.repeat(fitness, 4)[:, None])
    got = lax.all_to_all(payload, "pop", 0, 0, tiled=True)

    two_x = send(low_x, X_UP)
    far_high = send(far_y, X_DOWN)
    far_low = send(low_x, Y_SWAP)
    o1 = [own_o, swap(low_x), swap(high_x), swap(far_y)]

    e = [send(far_low[:112], X_UP), send(two_x[112:208], Y_SWAP), send(far_high[208:], X_DOWN)]
    o2 = [swap(two_x), swap(far_high), swap(far_low)]
    oe = [swap(v) for v in e]

    chip = lambda dy, dx: ((y + dy) % 2) * XS + (x + dx) % XS
    ints = lambda *v: jnp.stack([jnp.asarray(i, jnp.int32) for i in v])
    acc = group(
        4,
        ((0, 0), (1, 0), (2, 0), (3, 0)),
        ints(chip(0, 0), chip(0, -1), chip(0, 1), chip(1, 0), core),
        w,
        a,
        [shard, low_x, high_x, far_y],
        o1,
    )
    update = pl.pallas_call(
        update_kernel,
        out_shape=jax.ShapeDtypeStruct((SHARD, COLS), bf16),
        grid_spec=pltpu.PrefetchScalarGridSpec(
            num_scalar_prefetch=1,
            grid=(1,),
            in_specs=[pl.BlockSpec((POPS * LOW, PAY), lambda j, s: (0, 0))],
            out_specs=pl.BlockSpec((SHARD, COLS), lambda j, s: (0, 0)),
            scratch_shapes=[pltpu.VMEM((WIDE, COLS), f32)],
        ),
        compiler_params=pltpu.CompilerParams(vmem_limit_bytes=VMEM),
        cost_estimate=cost(2 * 512 * WIDE * COLS, 512 * PAY * 2 + SHARD * COLS * 2),
    )(ints(pop % 2), got.reshape(POPS * LOW, PAY))
    acc = group(
        3,
        ((0, 0), (1, 0), (2, 0)),
        ints(chip(0, 2), chip(1, 1), chip(1, -1), core),
        w,
        a,
        [two_x, far_high, far_low],
        o2,
        acc=acc,
    )
    act = group(
        1,
        ((0, 0), (0, 112), (0, 208)),
        ints(chip(1, 2), core, pop),
        w,
        a,
        e,
        oe,
        acc=acc,
        last=(b, member_of_row.reshape(1, ROWS)),
    )
    return (act.T, update)


def solution(mesh):
    placed = (
        P("pop", "tp"),
        P(None, "tp"),
        P("pop", None, None),
        P("pop", None, "tp"),
        P("pop"),
        P("pop"),
    )
    return jax.shard_map(
        body,
        mesh=mesh,
        in_specs=placed,
        out_specs=(P("pop", "tp"), P("pop", "tp")),
        check_vma=False,
    )
```

```python
import math

import jax
import jax.numpy as jnp
from jax import lax
from jax.experimental import pallas as pl
from jax.experimental.pallas import tpu as pltpu
from jax.sharding import PartitionSpec as P

perturb_scale = 0.5
f32, bf16 = jnp.float32, jnp.bfloat16

D, COLS, ROWS, SHARD = 5120, 1088, 1024, 320
CHIP = 2 * SHARD
LOW = 32
TALL = COLS + LOW
NB = 256
WIDE = 384
BCOLS = 1152
PAY = 2 * WIDE + BCOLS
POPS, ZS, XS = 16, 8, 4
LAST = CHIP + 128
MIB = 2**20

IN_VMEM = pl.BlockSpec(memory_space=pltpu.VMEM)
IN_SMEM = pl.BlockSpec(memory_space=pltpu.SMEM)
ANYWHERE = pl.BlockSpec(memory_space=pl.ANY)
IN_HBM = pl.BlockSpec(memory_space=pltpu.HBM)

TP = [(y, x, c) for y in range(2) for x in range(XS) for c in range(2)]


def tp_at(y, x, c):
    return ((y % 2) * XS + x % XS) * 2 + c % 2


X_UP = [(tp_at(y, x, c), tp_at(y, x + 1, c)) for y, x, c in TP]
X_DOWN = [(tp_at(y, x, c), tp_at(y, x - 1, c)) for y, x, c in TP]
Y_SWAP = [(tp_at(y, x, c), tp_at(y + 1, x, c)) for y, x, c in TP]
CORE_SWAP = [(tp_at(y, x, c), tp_at(y, x, c + 1)) for y, x, c in TP]


Z_GROUPS = [[z * 2 + yl for z in range(ZS)] for yl in range(2)]
PAIR_SWAP = [(p, p ^ 1) for p in range(POPS)]

NEAR = ((0, 0), (0, -1), (0, 1), (1, 0))
FAR = ((0, 2), (1, 1), (1, -1), (1, 2))


def kernel_call(kernel, args, in_specs, outs, out_specs, scratch, flops, nbytes, vmem, alias=None):
    return pl.pallas_call(
        kernel,
        out_shape=[jax.ShapeDtypeStruct(shape, dtype) for shape, dtype in outs],
        in_specs=in_specs,
        out_specs=out_specs,
        scratch_shapes=scratch,
        input_output_aliases=alias or {},
        compiler_params=pltpu.CompilerParams(vmem_limit_bytes=vmem * MIB),
        cost_estimate=pl.CostEstimate(
            flops=int(flops), bytes_accessed=int(nbytes), transcendentals=0
        ),
    )(*args)


def start_all(pairs, sem):
    handles = [pltpu.make_async_copy(src, dst, sem.at[i]) for i, (src, dst) in enumerate(pairs)]
    for h in handles:
        h.start()
    return handles


def core_now():
    return lax.rem(lax.axis_index("tp"), 2)


def pair_now():
    return lax.rem(lax.axis_index("pop"), 2)


def weights_kernel(steps, w, a, b_hbm, wx, b_t, sem):
    tp = lax.axis_index("tp")
    x, y = lax.rem(tp // 2, XS), tp // (2 * XS)
    used = len(steps) * CHIP
    more = wx.shape[1] > used
    pairs = [(b_hbm, b_t)] if more else []
    for k, (dy, dx) in enumerate(steps):
        chip = lax.rem(y + dy, 2) * XS + lax.rem(x + dx + XS, XS)
        col = pl.ds(pl.multiple_of(chip * CHIP, 128), CHIP)
        here = pl.ds(k * CHIP, CHIP)
        pairs.append((w.at[:, col], wx.at[pl.ds(0, COLS), here]))
        pairs.append((a.at[:, col], wx.at[pl.ds(COLS, LOW), here]))
    handles = start_all(pairs, sem)
    if more:
        handles.pop(0).wait()
        wx[:, used:] = jnp.zeros((TALL, wx.shape[1] - used), bf16)
        wx[:COLS, used : used + LOW] = b_t[...]
    for h in handles:
        h.wait()


def weights(steps, extra, w, a, b_t, vmem):
    width = len(steps) * CHIP + extra
    (wx,) = kernel_call(
        lambda *refs: weights_kernel(steps, *refs),
        (w, a, b_t),
        [IN_HBM, ANYWHERE, ANYWHERE],
        [((TALL, width), bf16)],
        [IN_VMEM],
        [pltpu.VMEM((COLS, LOW), bf16), pltpu.SemaphoreType.DMA((2 * len(steps) + 1,))],
        0,
        4 * TALL * width,
        vmem,
    )
    return wx


def token_pairs(places, mine, other, xs):
    core = core_now()
    pairs = []
    for start, m, o in zip(places, mine, other):
        size = m.shape[0]
        m_row = pl.multiple_of(start + core * SHARD, 16)
        o_row = pl.multiple_of(start + (1 - core) * SHARD, 16)
        pairs.append((m, xs.at[pl.ds(m_row, size), :]))
        pairs.append((o, xs.at[pl.ds(o_row, size), :]))
    return pairs


def part_kernel(n, first, *refs):
    wx, mine, other = refs[0], refs[1 : 1 + n], refs[1 + n : 1 + 2 * n]
    acc, out, xs, sem = (None, *refs[-3:]) if first else refs[-4:]
    for h in start_all(token_pairs([k * CHIP for k in range(n)], mine, other, xs), sem):
        h.wait()
    depth = n * CHIP
    for j in range(ROWS // NB):
        cols = slice(j * NB, (j + 1) * NB)
        part = jnp.dot(wx[:, :depth], xs[:, cols], preferred_element_type=f32)
        out[:, cols] = part if first else acc[:, cols] + part


def part_product(wx, mine, other, acc=None):
    n = len(mine)
    first = acc is None
    args = (wx, *mine, *other) + (() if first else (acc,))
    (out,) = kernel_call(
        lambda *refs: part_kernel(n, first, *refs),
        args,
        [IN_VMEM, IN_HBM if first else IN_VMEM] + [IN_VMEM] * (len(args) - 2),
        [((TALL, ROWS), f32)],
        [IN_VMEM],
        [pltpu.VMEM((n * CHIP, ROWS), bf16), pltpu.SemaphoreType.DMA((2 * n,))],
        2 * TALL * n * CHIP * ROWS,
        2 * n * CHIP * (TALL + ROWS),
        14,
    )
    return out


def last_kernel(places, wx, *refs):
    n = len(places)
    mine, other = refs[:n], refs[n : 2 * n]
    acc, member, out, xs, act, sem = refs[2 * n :]
    handles = start_all(token_pairs(places, mine, other, xs), sem)
    off = wx.shape[1] - LAST
    rank_row = lax.broadcasted_iota(jnp.int32, (LOW, ROWS), 0) >> 2
    owned = rank_row == member[...] - lax.axis_index("pop") * 8
    xs[CHIP + LOW :, :] = jnp.zeros((LAST - CHIP - LOW, ROWS), bf16)
    for h in handles:
        h.wait()
    low = acc[COLS:, :] + jnp.dot(
        wx[COLS:, off : off + CHIP], xs[:CHIP, :], preferred_element_type=f32
    )
    scaled = low * (perturb_scale / math.sqrt(D))
    xs[CHIP : CHIP + LOW, :] = jnp.where(owned, scaled, 0.0).astype(bf16)
    done = []
    for j in range(ROWS // NB):
        cols = slice(j * NB, (j + 1) * NB)
        v = acc[:COLS, cols] + jnp.dot(wx[:COLS, off:], xs[:, cols], preferred_element_type=f32)
        half = 0.5 * v
        act[:, cols] = (half + half * jnp.tanh(half)).astype(bf16)
        copy = pltpu.make_async_copy(act.at[:, cols], out.at[:, cols], sem.at[2 * n + j])
        copy.start()
        done.append(copy)
    for copy in done:
        copy.wait()


def last_product(places, wx, mine, other, acc, member):
    n = len(places)
    args = (wx, *mine, *other, acc, member)
    (out,) = kernel_call(
        lambda *refs: last_kernel(places, *refs),
        args,
        [IN_VMEM] * len(args),
        [((COLS, ROWS), bf16)],
        [IN_HBM],
        [
            pltpu.VMEM((LAST, ROWS), bf16),
            pltpu.VMEM((COLS, ROWS), bf16),
            pltpu.SemaphoreType.DMA((2 * n + ROWS // NB,)),
        ],
        2 * TALL * CHIP * ROWS,
        2 * CHIP * (TALL + ROWS),
        12,
    )
    return out


def slices_for(pair, z):
    return pl.ds(pl.multiple_of(2 * SHARD * z + 256 * pair, 128), WIDE)


def factors_kernel(rank, a_hbm, b_hbm, a_flat, b_t, out, a, b, wide_a, wide_b, wide_s, sem):
    for h in start_all([(a_hbm, a), (b_hbm, b)], sem):
        h.wait()
    wide_s[:, BCOLS - 128 :] = jnp.zeros((LOW, 128), f32)
    for m in range(8):
        rows = slice(4 * m, 4 * m + 4)
        wide_a[rows, :] = a[m].astype(f32)
        bm = b[m].astype(f32)
        wide_b[rows, :] = bm
        fitness = 2.0 * jnp.full((4, COLS), rank[m], jnp.int32).astype(f32) / 127.0 - 1.0
        wide_s[rows, :COLS] = bm * fitness
    a_flat[...] = wide_a[...].astype(bf16)
    b_t[...] = wide_b[...].T.astype(bf16)
    scaled = wide_s[...].astype(bf16)
    pair = pair_now()
    for z in range(ZS):
        out[z, :, :WIDE] = a_flat[:, slices_for(pair, z)]
        out[z, :, WIDE : 2 * WIDE] = a_flat[:, slices_for(1 - pair, z)]
        out[z, :, 2 * WIDE :] = scaled


def pair_kernel(got, out):
    out[...] = got[:, WIDE:]


def pair_message(got):
    shape = (got.shape[0], PAY - WIDE)
    (out,) = kernel_call(
        pair_kernel, (got,), [IN_VMEM], [(shape, bf16)], [IN_VMEM], [], 0, 4 * math.prod(shape), 4
    )
    return out


def update_kernel(got, far, out, wide, up, sem):
    def outer(left, right):
        return lax.dot_general(
            left, right, (((0,), (0,)), ((), ())), preferred_element_type=f32
        )

    wide[...] = (
        outer(got[:, :WIDE], got[:, 2 * WIDE : 2 * WIDE + COLS])
        + outer(far[:, :WIDE], far[:, WIDE : WIDE + COLS])
    )
    first = pl.multiple_of(pair_now() * 64, 64)
    up[...] = (wide[pl.ds(first, SHARD), :] * (1.0 / math.sqrt(512))).astype(bf16)
    copy = pltpu.make_async_copy(up, out, sem)
    copy.start()
    copy.wait()


def body(tokens, weight, factor_a, factor_b, member_of_row, fitness_rank):
    shard = tokens.T
    w = weight.T

    send = lambda v, perm: lax.ppermute(v, "tp", perm)
    swap = lambda v: send(v, CORE_SWAP)

    low_x = send(shard, X_UP)
    high_x = send(shard, X_DOWN)
    far_y = send(shard, Y_SWAP)
    own_o = swap(shard)

    a, b_t, payload = kernel_call(
        factors_kernel,
        (fitness_rank, factor_a, factor_b),
        [IN_SMEM, IN_HBM, IN_HBM],
        [((LOW, D), bf16), ((COLS, LOW), bf16), ((ZS, LOW, PAY), bf16)],
        [IN_VMEM] * 3,
        [
            pltpu.VMEM((8, 4, D), bf16),
            pltpu.VMEM((8, 4, COLS), bf16),
            pltpu.VMEM((LOW, D), f32),
            pltpu.VMEM((LOW, COLS), f32),
            pltpu.VMEM((LOW, BCOLS), f32),
            pltpu.SemaphoreType.DMA((2,)),
        ],
        0,
        2 * LOW * (D + COLS + ZS * PAY),
        54,
    )
    got = lax.all_to_all(payload, "pop", 0, 0, axis_index_groups=Z_GROUPS, tiled=True)
    got = got.reshape(ZS * LOW, PAY)

    near_w = weights(NEAR, 0, w, a, b_t, 44)
    far_w = weights(FAR, 128, w, a, b_t, 42)

    two_x = send(low_x, X_UP)
    far_high = send(far_y, X_DOWN)
    far_low = send(low_x, Y_SWAP)
    o1 = [own_o, swap(low_x), swap(high_x), swap(far_y)]
    acc = part_product(near_w, [shard, low_x, high_x, far_y], o1)

    two_x, far_high, far_low, acc, got = lax.optimization_barrier(
        (two_x, far_high, far_low, acc, got)
    )
    e = [send(far_low[: SHARD // 2], X_UP), send(far_high[SHARD // 2 :], X_DOWN)]
    o2 = [swap(two_x), swap(far_high), swap(far_low)]
    far = lax.ppermute(pair_message(got), "pop", PAIR_SWAP)
    acc = part_product(far_w, [two_x, far_high, far_low], o2, acc)

    *e, acc = lax.optimization_barrier((*e, acc))
    oe = [swap(v) for v in e]
    act = last_product((0, SHARD // 2), far_w, e, oe, acc, member_of_row.reshape(1, ROWS))
    act, far = lax.optimization_barrier((act, far))
    (update,) = kernel_call(
        update_kernel,
        (got, far),
        [IN_VMEM] * 2,
        [((SHARD, COLS), bf16)],
        [IN_HBM],
        [
            pltpu.VMEM((WIDE, COLS), f32),
            pltpu.VMEM((SHARD, COLS), bf16),
            pltpu.SemaphoreType.DMA,
        ],
        2 * 512 * WIDE * COLS,
        2 * 512 * PAY,
        8,
    )
    return (act.T, update)


def solution(mesh):
    placed = (
        P("pop", "tp"),
        P(None, "tp"),
        P("pop", None, None),
        P("pop", None, "tp"),
        P("pop"),
        P("pop"),
    )
    return jax.shard_map(
        body,
        mesh=mesh,
        in_specs=placed,
        out_specs=(P("pop", "tp"), P("pop", "tp")),
        check_vma=False,
    )
```

```python
import math

import jax
import jax.numpy as jnp
from jax import lax
from jax.experimental import pallas as pl
from jax.experimental.pallas import tpu as pltpu
from jax.sharding import PartitionSpec as P

perturb_scale = 0.5
f32, bf16 = jnp.float32, jnp.bfloat16

D, COLS, ROWS, SHARD = 5120, 1088, 1024, 320
CHIP = 2 * SHARD
LOW = 32
TALL = COLS + LOW
NB = 256
WIDE = 384
BCOLS = 1152
PAY = 2 * WIDE + BCOLS
POPS, ZS, XS = 16, 8, 4
LAST = CHIP + 128
MIB = 2**20

IN_VMEM = pl.BlockSpec(memory_space=pltpu.VMEM)
IN_SMEM = pl.BlockSpec(memory_space=pltpu.SMEM)
ANYWHERE = pl.BlockSpec(memory_space=pl.ANY)
IN_HBM = pl.BlockSpec(memory_space=pltpu.HBM)

TP = [(y, x, c) for y in range(2) for x in range(XS) for c in range(2)]


def tp_at(y, x, c):
    return ((y % 2) * XS + x % XS) * 2 + c % 2


X_UP = [(tp_at(y, x, c), tp_at(y, x + 1, c)) for y, x, c in TP]
X_DOWN = [(tp_at(y, x, c), tp_at(y, x - 1, c)) for y, x, c in TP]
Y_SWAP = [(tp_at(y, x, c), tp_at(y + 1, x, c)) for y, x, c in TP]
CORE_SWAP = [(tp_at(y, x, c), tp_at(y, x, c + 1)) for y, x, c in TP]


Z_GROUPS = [[z * 2 + yl for z in range(ZS)] for yl in range(2)]
PAIR_SWAP = [(p, p ^ 1) for p in range(POPS)]

NEAR = ((0, 0), (0, -1), (0, 1), (1, 0))
FAR = ((0, 2), (1, 1), (1, -1), (1, 2))


def kernel_call(kernel, args, in_specs, outs, out_specs, scratch, flops, nbytes, vmem, alias=None):
    return pl.pallas_call(
        kernel,
        out_shape=[jax.ShapeDtypeStruct(shape, dtype) for shape, dtype in outs],
        in_specs=in_specs,
        out_specs=out_specs,
        scratch_shapes=scratch,
        input_output_aliases=alias or {},
        compiler_params=pltpu.CompilerParams(vmem_limit_bytes=vmem * MIB),
        cost_estimate=pl.CostEstimate(
            flops=int(flops), bytes_accessed=int(nbytes), transcendentals=0
        ),
    )(*args)


def start_all(pairs, sem):
    handles = [pltpu.make_async_copy(src, dst, sem.at[i]) for i, (src, dst) in enumerate(pairs)]
    for h in handles:
        h.start()
    return handles


def core_now():
    return lax.rem(lax.axis_index("tp"), 2)


def pair_now():
    return lax.rem(lax.axis_index("pop"), 2)


def weights_kernel(steps, w, a, *refs):
    more = len(refs) > 2
    wx, sem = (refs[1], refs[3]) if more else refs
    tp = lax.axis_index("tp")
    x, y = lax.rem(tp // 2, XS), tp // (2 * XS)
    used = len(steps) * CHIP
    pairs = [(refs[0], refs[2])] if more else []
    for k, (dy, dx) in enumerate(steps):
        chip = lax.rem(y + dy, 2) * XS + lax.rem(x + dx + XS, XS)
        col = pl.ds(pl.multiple_of(chip * CHIP, 128), CHIP)
        here = pl.ds(k * CHIP, CHIP)
        pairs.append((w.at[:, col], wx.at[pl.ds(0, COLS), here]))
        pairs.append((a.at[:, col], wx.at[pl.ds(COLS, LOW), here]))
    handles = start_all(pairs, sem)
    if more:
        handles.pop(0).wait()
        wx[:, used:] = jnp.zeros((TALL, wx.shape[1] - used), bf16)
        wx[:COLS, used : used + LOW] = refs[2][...]
    for h in handles:
        h.wait()


def weights(steps, extra, w, a, vmem, b_t=None):
    more = b_t is not None
    width = len(steps) * CHIP + extra
    (wx,) = kernel_call(
        lambda *refs: weights_kernel(steps, *refs),
        (w, a) + ((b_t,) if more else ()),
        [IN_HBM] + [ANYWHERE] * (2 if more else 1),
        [((TALL, width), bf16)],
        [IN_VMEM],
        ([pltpu.VMEM((COLS, LOW), bf16)] if more else [])
        + [pltpu.SemaphoreType.DMA((2 * len(steps) + 1,))],
        0,
        4 * TALL * width,
        vmem,
    )
    return wx


def token_pairs(places, mine, other, xs):
    core = core_now()
    pairs = []
    for start, m, o in zip(places, mine, other):
        size = m.shape[0]
        m_row = pl.multiple_of(start + core * SHARD, 16)
        o_row = pl.multiple_of(start + (1 - core) * SHARD, 16)
        pairs.append((m, xs.at[pl.ds(m_row, size), :]))
        pairs.append((o, xs.at[pl.ds(o_row, size), :]))
    return pairs


def part_kernel(n, first, *refs):
    wx, mine, other = refs[0], refs[1 : 1 + n], refs[1 + n : 1 + 2 * n]
    acc, out, xs, sem = (None, *refs[-3:]) if first else refs[-4:]
    depth = n * CHIP
    for h in start_all(token_pairs([k * CHIP for k in range(n)], mine, other, xs), sem):
        h.wait()
    for j in range(ROWS // NB):
        cols = slice(j * NB, (j + 1) * NB)
        part = jnp.dot(wx[:, :depth], xs[:, cols], preferred_element_type=f32)
        out[:, cols] = part if first else acc[:, cols] + part


def part_product(wx, mine, other, acc=None):
    n = len(mine)
    first = acc is None
    args = (wx, *mine, *other) + (() if first else (acc,))
    (out,) = kernel_call(
        lambda *refs: part_kernel(n, first, *refs),
        args,
        [IN_VMEM, IN_HBM if first else IN_VMEM] + [IN_VMEM] * (len(args) - 2),
        [((TALL, ROWS), f32)],
        [IN_VMEM],
        [
            pltpu.VMEM((n * CHIP, ROWS), bf16),
            pltpu.SemaphoreType.DMA((2 * n,)),
        ],
        2 * TALL * n * CHIP * ROWS,
        2 * n * CHIP * (TALL + ROWS),
        14,
    )
    return out


def last_kernel(places, wx, *refs):
    n = len(places)
    mine, other = refs[:n], refs[n : 2 * n]
    acc, member, out, xs, act, sem = refs[2 * n :]
    handles = start_all(token_pairs(places, mine, other, xs), sem)
    off = wx.shape[1] - LAST
    rank_row = lax.broadcasted_iota(jnp.int32, (LOW, ROWS), 0) >> 2
    owned = rank_row == member[...] - lax.axis_index("pop") * 8
    xs[CHIP + LOW :, :] = jnp.zeros((LAST - CHIP - LOW, ROWS), bf16)
    for h in handles:
        h.wait()
    low = acc[COLS:, :] + jnp.dot(
        wx[COLS:, off : off + CHIP], xs[:CHIP, :], preferred_element_type=f32
    )
    scaled = low * (perturb_scale / math.sqrt(D))
    xs[CHIP : CHIP + LOW, :] = jnp.where(owned, scaled, 0.0).astype(bf16)
    done = []
    for j in range(ROWS // NB):
        cols = slice(j * NB, (j + 1) * NB)
        v = acc[:COLS, cols] + jnp.dot(wx[:COLS, off:], xs[:, cols], preferred_element_type=f32)
        half = 0.5 * v
        act[:, cols] = (half + half * jnp.tanh(half)).astype(bf16)
        copy = pltpu.make_async_copy(act.at[:, cols], out.at[:, cols], sem.at[2 * n + j])
        copy.start()
        done.append(copy)
    for copy in done:
        copy.wait()


def last_product(places, wx, mine, other, acc, member):
    n = len(places)
    args = (wx, *mine, *other, acc, member)
    (out,) = kernel_call(
        lambda *refs: last_kernel(places, *refs),
        args,
        [IN_VMEM] * len(args),
        [((COLS, ROWS), bf16)],
        [IN_HBM],
        [
            pltpu.VMEM((LAST, ROWS), bf16),
            pltpu.VMEM((COLS, ROWS), bf16),
            pltpu.SemaphoreType.DMA((2 * n + ROWS // NB,)),
        ],
        2 * TALL * CHIP * ROWS,
        2 * CHIP * (TALL + ROWS),
        12,
    )
    return out


def slices_for(pair, z):
    return pl.ds(pl.multiple_of(2 * SHARD * z + 256 * pair, 128), WIDE)


def factors_kernel(rank, a_hbm, b_hbm, a_flat, b_t, out, a, b, wide_a, wide_b, wide_s, sem):
    for h in start_all([(a_hbm, a), (b_hbm, b)], sem):
        h.wait()
    wide_s[:, BCOLS - 128 :] = jnp.zeros((LOW, 128), f32)
    for m in range(8):
        rows = slice(4 * m, 4 * m + 4)
        wide_a[rows, :] = a[m].astype(f32)
        bm = b[m].astype(f32)
        wide_b[rows, :] = bm
        fitness = 2.0 * jnp.full((4, COLS), rank[m], jnp.int32).astype(f32) / 127.0 - 1.0
        wide_s[rows, :COLS] = bm * fitness
    a_flat[...] = wide_a[...].astype(bf16)
    b_t[...] = wide_b[...].T.astype(bf16)
    scaled = wide_s[...].astype(bf16)
    pair = pair_now()
    for z in range(ZS):
        out[z, :, :WIDE] = a_flat[:, slices_for(pair, z)]
        out[z, :, WIDE : 2 * WIDE] = a_flat[:, slices_for(1 - pair, z)]
        out[z, :, 2 * WIDE :] = scaled


def pair_kernel(got, out):
    there = got[:, WIDE : 2 * WIDE].astype(f32)
    odd = jnp.full((got.shape[0], SHARD), pair_now(), jnp.int32) == 0
    out[:, :COLS] = got[:, 2 * WIDE : 2 * WIDE + COLS]
    out[:, COLS:] = jnp.where(odd, there[:, 64:], there[:, :SHARD]).astype(bf16)


def pair_message(got):
    shape = (got.shape[0], COLS + SHARD)
    (out,) = kernel_call(
        pair_kernel, (got,), [IN_VMEM], [(shape, bf16)], [IN_VMEM], [], 0, 4 * math.prod(shape), 4
    )
    return out


def outer(left, right):
    return lax.dot_general(left, right, (((0,), (0,)), ((), ())), preferred_element_type=f32)


def own_update_kernel(got, out):
    out[...] = outer(got[:, :WIDE], got[:, 2 * WIDE : 2 * WIDE + COLS])


def update_kernel(own, far, out, up, sem):
    first = pl.multiple_of(pair_now() * 64, 64)
    total = own[pl.ds(first, SHARD), :] + outer(far[:, COLS:], far[:, :COLS])
    up[...] = (total * (1.0 / math.sqrt(512))).astype(bf16)
    copy = pltpu.make_async_copy(up, out, sem)
    copy.start()
    copy.wait()


def body(tokens, weight, factor_a, factor_b, member_of_row, fitness_rank):
    shard = tokens.T
    w = weight.T

    send = lambda v, perm: lax.ppermute(v, "tp", perm)
    swap = lambda v: send(v, CORE_SWAP)

    low_x = send(shard, X_UP)
    high_x = send(shard, X_DOWN)
    far_y = send(shard, Y_SWAP)
    own_o = swap(shard)

    a, b_t, payload = kernel_call(
        factors_kernel,
        (fitness_rank, factor_a, factor_b),
        [IN_SMEM, IN_HBM, IN_HBM],
        [((LOW, D), bf16), ((COLS, LOW), bf16), ((ZS, LOW, PAY), bf16)],
        [IN_VMEM] * 3,
        [
            pltpu.VMEM((8, 4, D), bf16),
            pltpu.VMEM((8, 4, COLS), bf16),
            pltpu.VMEM((LOW, D), f32),
            pltpu.VMEM((LOW, COLS), f32),
            pltpu.VMEM((LOW, BCOLS), f32),
            pltpu.SemaphoreType.DMA((2,)),
        ],
        0,
        2 * LOW * (D + COLS + ZS * PAY),
        54,
    )
    got = lax.all_to_all(payload, "pop", 0, 0, axis_index_groups=Z_GROUPS, tiled=True)
    got = got.reshape(ZS * LOW, PAY)

    near_w = weights(NEAR, 0, w, a, 44)
    two_x = send(low_x, X_UP)
    far_high = send(far_y, X_DOWN)
    far_low = send(low_x, Y_SWAP)
    o1 = [own_o, swap(low_x), swap(high_x), swap(far_y)]
    acc = part_product(near_w, [shard, low_x, high_x, far_y], o1)

    two_x, far_high, far_low, acc, got = lax.optimization_barrier(
        (two_x, far_high, far_low, acc, got)
    )
    message, far_low, far_high = lax.optimization_barrier(
        (pair_message(got), far_low, far_high)
    )
    e = [send(far_low[: SHARD // 2], X_UP), send(far_high[SHARD // 2 :], X_DOWN)]
    o2 = [swap(two_x), swap(far_high), swap(far_low)]
    far = lax.ppermute(message, "pop", PAIR_SWAP)
    o2[0], b_t = lax.optimization_barrier((o2[0], b_t))
    far_w = weights(FAR, 128, w, a, 42, b_t)
    acc = part_product(far_w, [two_x, far_high, far_low], o2, acc)

    *e, acc, got = lax.optimization_barrier((*e, acc, got))
    oe = [swap(v) for v in e]
    (own,) = kernel_call(
        own_update_kernel,
        (got,),
        [IN_VMEM],
        [((WIDE, COLS), f32)],
        [IN_VMEM],
        [],
        2 * 256 * WIDE * COLS,
        2 * 256 * PAY,
        6,
    )
    acc, own = lax.optimization_barrier((acc, own))
    act = last_product((0, SHARD // 2), far_w, e, oe, acc, member_of_row.reshape(1, ROWS))
    act, far = lax.optimization_barrier((act, far))
    (update,) = kernel_call(
        update_kernel,
        (own, far),
        [IN_VMEM] * 2,
        [((SHARD, COLS), bf16)],
        [IN_HBM],
        [
            pltpu.VMEM((SHARD, COLS), bf16),
            pltpu.SemaphoreType.DMA,
        ],
        2 * 512 * WIDE * COLS,
        2 * 512 * PAY,
        8,
    )
    return (act.T, update)


def solution(mesh):
    placed = (
        P("pop", "tp"),
        P(None, "tp"),
        P("pop", None, None),
        P("pop", None, "tp"),
        P("pop"),
        P("pop"),
    )
    return jax.shard_map(
        body,
        mesh=mesh,
        in_specs=placed,
        out_specs=(P("pop", "tp"), P("pop", "tp")),
        check_vma=False,
    )
```

```python
import math

import jax
import jax.numpy as jnp
from jax import lax
from jax.experimental import pallas as pl
from jax.experimental.pallas import tpu as pltpu
from jax.sharding import PartitionSpec as P

perturb_scale = 0.5
f32, bf16 = jnp.float32, jnp.bfloat16

D, COLS, ROWS, SHARD = 5120, 1088, 1024, 320
CHIP = 2 * SHARD
LOW = 32
TALL = COLS + LOW
NB = 256
WIDE = 384
BCOLS = 1152
PAY = 2 * WIDE + BCOLS
POPS, ZS, XS = 16, 8, 4
LAST = CHIP + 128
MIB = 2**20

IN_VMEM = pl.BlockSpec(memory_space=pltpu.VMEM)
IN_SMEM = pl.BlockSpec(memory_space=pltpu.SMEM)
ANYWHERE = pl.BlockSpec(memory_space=pl.ANY)
IN_HBM = pl.BlockSpec(memory_space=pltpu.HBM)

TP = [(y, x, c) for y in range(2) for x in range(XS) for c in range(2)]


def tp_at(y, x, c):
    return ((y % 2) * XS + x % XS) * 2 + c % 2


X_UP = [(tp_at(y, x, c), tp_at(y, x + 1, c)) for y, x, c in TP]
X_DOWN = [(tp_at(y, x, c), tp_at(y, x - 1, c)) for y, x, c in TP]
Y_SWAP = [(tp_at(y, x, c), tp_at(y + 1, x, c)) for y, x, c in TP]
CORE_SWAP = [(tp_at(y, x, c), tp_at(y, x, c + 1)) for y, x, c in TP]


Z_GROUPS = [[z * 2 + yl for z in range(ZS)] for yl in range(2)]
PAIR_SWAP = [(p, p ^ 1) for p in range(POPS)]

NEAR = ((0, 0), (0, -1), (0, 1), (1, 0))
FAR = ((0, 2), (1, 1), (1, -1), (1, 2))


def kernel_call(kernel, args, in_specs, outs, out_specs, scratch, flops, nbytes, vmem, alias=None):
    return pl.pallas_call(
        kernel,
        out_shape=[jax.ShapeDtypeStruct(shape, dtype) for shape, dtype in outs],
        in_specs=in_specs,
        out_specs=out_specs,
        scratch_shapes=scratch,
        input_output_aliases=alias or {},
        compiler_params=pltpu.CompilerParams(vmem_limit_bytes=vmem * MIB),
        cost_estimate=pl.CostEstimate(
            flops=int(flops), bytes_accessed=int(nbytes), transcendentals=0
        ),
    )(*args)


def start_all(pairs, sem):
    handles = [pltpu.make_async_copy(src, dst, sem.at[i]) for i, (src, dst) in enumerate(pairs)]
    for h in handles:
        h.start()
    return handles


def core_now():
    return lax.rem(lax.axis_index("tp"), 2)


def pair_now():
    return lax.rem(lax.axis_index("pop"), 2)


def weights_kernel(steps, w, a, *refs):
    more = len(refs) > 2
    wx, sem = (refs[1], refs[3]) if more else refs
    tp = lax.axis_index("tp")
    x, y = lax.rem(tp // 2, XS), tp // (2 * XS)
    used = len(steps) * CHIP
    pairs = [(refs[0], refs[2])] if more else []
    for k, (dy, dx) in enumerate(steps):
        chip = lax.rem(y + dy, 2) * XS + lax.rem(x + dx + XS, XS)
        col = pl.ds(pl.multiple_of(chip * CHIP, 128), CHIP)
        here = pl.ds(k * CHIP, CHIP)
        pairs.append((w.at[:, col], wx.at[pl.ds(0, COLS), here]))
        pairs.append((a.at[:, col], wx.at[pl.ds(COLS, LOW), here]))
    handles = start_all(pairs, sem)
    if more:
        handles.pop(0).wait()
        wx[:, used:] = jnp.zeros((TALL, wx.shape[1] - used), bf16)
        wx[:COLS, used : used + LOW] = refs[2][...]
    for h in handles:
        h.wait()


def weights(steps, extra, w, a, vmem, b_t=None):
    more = b_t is not None
    width = len(steps) * CHIP + extra
    (wx,) = kernel_call(
        lambda *refs: weights_kernel(steps, *refs),
        (w, a) + ((b_t,) if more else ()),
        [IN_HBM] + [ANYWHERE] * (2 if more else 1),
        [((TALL, width), bf16)],
        [IN_VMEM],
        ([pltpu.VMEM((COLS, LOW), bf16)] if more else [])
        + [pltpu.SemaphoreType.DMA((2 * len(steps) + 1,))],
        0,
        4 * TALL * width,
        vmem,
    )
    return wx


def token_pairs(places, mine, other, xs):
    core = core_now()
    pairs = []
    for start, m, o in zip(places, mine, other):
        size = m.shape[0]
        m_row = pl.multiple_of(start + core * SHARD, 16)
        o_row = pl.multiple_of(start + (1 - core) * SHARD, 16)
        pairs.append((m, xs.at[pl.ds(m_row, size), :]))
        pairs.append((o, xs.at[pl.ds(o_row, size), :]))
    return pairs


def part_kernel(n, first, *refs):
    wx, mine, other = refs[0], refs[1 : 1 + n], refs[1 + n : 1 + 2 * n]
    acc, out, xs, sem = (None, *refs[-3:]) if first else refs[-4:]
    depth = n * CHIP
    for h in start_all(token_pairs([k * CHIP for k in range(n)], mine, other, xs), sem):
        h.wait()
    for j in range(ROWS // NB):
        cols = slice(j * NB, (j + 1) * NB)
        part = jnp.dot(wx[:, :depth], xs[:, cols], preferred_element_type=f32)
        out[:, cols] = part if first else acc[:, cols] + part


def part_product(wx, mine, other, acc=None):
    n = len(mine)
    first = acc is None
    args = (wx, *mine, *other) + (() if first else (acc,))
    (out,) = kernel_call(
        lambda *refs: part_kernel(n, first, *refs),
        args,
        [IN_VMEM, IN_HBM if first else IN_VMEM] + [IN_VMEM] * (len(args) - 2),
        [((TALL, ROWS), f32)],
        [IN_VMEM],
        [
            pltpu.VMEM((n * CHIP, ROWS), bf16),
            pltpu.SemaphoreType.DMA((2 * n,)),
        ],
        2 * TALL * n * CHIP * ROWS,
        2 * n * CHIP * (TALL + ROWS),
        14,
    )
    return out


def last_kernel(places, wx, *refs):
    n = len(places)
    mine, other = refs[:n], refs[n : 2 * n]
    acc, member, out, xs, act, sem = refs[2 * n :]
    handles = start_all(token_pairs(places, mine, other, xs), sem)
    off = wx.shape[1] - LAST
    rank_row = lax.broadcasted_iota(jnp.int32, (LOW, ROWS), 0) >> 2
    owned = rank_row == member[...] - lax.axis_index("pop") * 8
    xs[CHIP + LOW :, :] = jnp.zeros((LAST - CHIP - LOW, ROWS), bf16)
    for h in handles:
        h.wait()
    low = acc[COLS:, :] + jnp.dot(
        wx[COLS:, off : off + CHIP], xs[:CHIP, :], preferred_element_type=f32
    )
    scaled = low * (perturb_scale / math.sqrt(D))
    xs[CHIP : CHIP + LOW, :] = jnp.where(owned, scaled, 0.0).astype(bf16)
    done = []
    for j in range(ROWS // NB):
        cols = slice(j * NB, (j + 1) * NB)
        v = acc[:COLS, cols] + jnp.dot(wx[:COLS, off:], xs[:, cols], preferred_element_type=f32)
        half = 0.5 * v
        act[:, cols] = (half + half * jnp.tanh(half)).astype(bf16)
        copy = pltpu.make_async_copy(act.at[:, cols], out.at[:, cols], sem.at[2 * n + j])
        copy.start()
        done.append(copy)
    for copy in done:
        copy.wait()


def last_product(places, wx, mine, other, acc, member):
    n = len(places)
    args = (wx, *mine, *other, acc, member)
    (out,) = kernel_call(
        lambda *refs: last_kernel(places, *refs),
        args,
        [IN_VMEM] * len(args),
        [((COLS, ROWS), bf16)],
        [IN_HBM],
        [
            pltpu.VMEM((LAST, ROWS), bf16),
            pltpu.VMEM((COLS, ROWS), bf16),
            pltpu.SemaphoreType.DMA((2 * n + ROWS // NB,)),
        ],
        2 * TALL * CHIP * ROWS,
        2 * CHIP * (TALL + ROWS),
        12,
    )
    return out


def slices_for(pair, z):
    return pl.ds(pl.multiple_of(2 * SHARD * z + 256 * pair, 128), WIDE)


def factors_kernel(rank, a_hbm, b_hbm, a_flat, b_t, out, a, b, wide_a, wide_b, wide_s, sem):
    for h in start_all([(a_hbm, a), (b_hbm, b)], sem):
        h.wait()
    wide_s[:, BCOLS - 128 :] = jnp.zeros((LOW, 128), f32)
    for m in range(8):
        rows = slice(4 * m, 4 * m + 4)
        wide_a[rows, :] = a[m].astype(f32)
        bm = b[m].astype(f32)
        wide_b[rows, :] = bm
        fitness = 2.0 * jnp.full((4, COLS), rank[m], jnp.int32).astype(f32) / 127.0 - 1.0
        wide_s[rows, :COLS] = bm * fitness
    a_flat[...] = wide_a[...].astype(bf16)
    b_t[...] = wide_b[...].T.astype(bf16)
    scaled = wide_s[...].astype(bf16)
    pair = pair_now()
    for z in range(ZS):
        out[z, :, :WIDE] = a_flat[:, slices_for(pair, z)]
        out[z, :, WIDE : 2 * WIDE] = a_flat[:, slices_for(1 - pair, z)]
        out[z, :, 2 * WIDE :] = scaled


def pair_kernel(got, low, high, out, low_half, high_half):
    low_half[...] = low[: SHARD // 2, :]
    high_half[...] = high[SHARD // 2 :, :]
    there = got[:, WIDE : 2 * WIDE].astype(f32)
    odd = jnp.full((got.shape[0], SHARD), pair_now(), jnp.int32) == 0
    out[:, :COLS] = got[:, 2 * WIDE : 2 * WIDE + COLS]
    out[:, COLS:] = jnp.where(odd, there[:, 64:], there[:, :SHARD]).astype(bf16)


def pair_message(got, low, high):
    shape = (got.shape[0], COLS + SHARD)
    half = (SHARD // 2, ROWS)
    return kernel_call(
        pair_kernel,
        (got, low, high),
        [IN_VMEM] * 3,
        [(shape, bf16), (half, bf16), (half, bf16)],
        [IN_VMEM] * 3,
        [],
        0,
        4 * math.prod(shape),
        4,
    )


def outer(left, right):
    return lax.dot_general(left, right, (((0,), (0,)), ((), ())), preferred_element_type=f32)


def own_update_kernel(got, out):
    out[...] = outer(got[:, :WIDE], got[:, 2 * WIDE : 2 * WIDE + COLS])


def update_kernel(own, far, out, up, sem):
    first = pl.multiple_of(pair_now() * 64, 64)
    total = own[pl.ds(first, SHARD), :] + outer(far[:, COLS:], far[:, :COLS])
    up[...] = (total * (1.0 / math.sqrt(512))).astype(bf16)
    copy = pltpu.make_async_copy(up, out, sem)
    copy.start()
    copy.wait()


def body(tokens, weight, factor_a, factor_b, member_of_row, fitness_rank):
    shard = tokens.T
    w = weight.T

    send = lambda v, perm: lax.ppermute(v, "tp", perm)
    swap = lambda v: send(v, CORE_SWAP)

    low_x = send(shard, X_UP)
    high_x = send(shard, X_DOWN)
    far_y = send(shard, Y_SWAP)
    own_o = swap(shard)

    a, b_t, payload = kernel_call(
        factors_kernel,
        (fitness_rank, factor_a, factor_b),
        [IN_SMEM, IN_HBM, IN_HBM],
        [((LOW, D), bf16), ((COLS, LOW), bf16), ((ZS, LOW, PAY), bf16)],
        [IN_VMEM] * 3,
        [
            pltpu.VMEM((8, 4, D), bf16),
            pltpu.VMEM((8, 4, COLS), bf16),
            pltpu.VMEM((LOW, D), f32),
            pltpu.VMEM((LOW, COLS), f32),
            pltpu.VMEM((LOW, BCOLS), f32),
            pltpu.SemaphoreType.DMA((2,)),
        ],
        0,
        2 * LOW * (D + COLS + ZS * PAY),
        54,
    )
    got = lax.all_to_all(payload, "pop", 0, 0, axis_index_groups=Z_GROUPS, tiled=True)
    got = got.reshape(ZS * LOW, PAY)

    near_w = weights(NEAR, 0, w, a, 44)
    two_x = send(low_x, X_UP)
    far_high = send(far_y, X_DOWN)
    far_low = send(low_x, Y_SWAP)
    o1 = [own_o, swap(low_x), swap(high_x), swap(far_y)]
    acc = part_product(near_w, [shard, low_x, high_x, far_y], o1)

    two_x, far_high, far_low, acc, got = lax.optimization_barrier(
        (two_x, far_high, far_low, acc, got)
    )
    message, low_half, high_half = pair_message(got, far_low, far_high)
    e = [send(low_half, X_UP), send(high_half, X_DOWN)]
    o2 = [swap(two_x), swap(far_high), swap(far_low)]
    far = lax.ppermute(message, "pop", PAIR_SWAP)
    o2[0], b_t = lax.optimization_barrier((o2[0], b_t))
    far_w = weights(FAR, 128, w, a, 42, b_t)
    acc = part_product(far_w, [two_x, far_high, far_low], o2, acc)

    *e, acc, got = lax.optimization_barrier((*e, acc, got))
    oe = [swap(v) for v in e]
    (own,) = kernel_call(
        own_update_kernel,
        (got,),
        [IN_VMEM],
        [((WIDE, COLS), f32)],
        [IN_VMEM],
        [],
        2 * 256 * WIDE * COLS,
        2 * 256 * PAY,
        6,
    )
    acc, own = lax.optimization_barrier((acc, own))
    act = last_product((0, SHARD // 2), far_w, e, oe, acc, member_of_row.reshape(1, ROWS))
    act, far = lax.optimization_barrier((act, far))
    (update,) = kernel_call(
        update_kernel,
        (own, far),
        [IN_VMEM] * 2,
        [((SHARD, COLS), bf16)],
        [IN_HBM],
        [
            pltpu.VMEM((SHARD, COLS), bf16),
            pltpu.SemaphoreType.DMA,
        ],
        2 * 512 * WIDE * COLS,
        2 * 512 * PAY,
        8,
    )
    return (act.T, update)


def solution(mesh):
    placed = (
        P("pop", "tp"),
        P(None, "tp"),
        P("pop", None, None),
        P("pop", None, "tp"),
        P("pop"),
        P("pop"),
    )
    return jax.shard_map(
        body,
        mesh=mesh,
        in_specs=placed,
        out_specs=(P("pop", "tp"), P("pop", "tp")),
        check_vma=False,
    )
```
